256 devices in a mesh: ctx: 64 (over y, z_hi, x, core), hg: 4 (over z_lo).
Axes of the slice: x: 4, y: 4, z: 8 (z_hi: 2, z_lo: 4; z = z_hi * 4 + z_lo), core: 2. Of those that a mesh axis runs over, the one named last changes fastest.
Arguments:
- main_query: bfloat16 [256, 24576], P('ctx', 'hg'), may hold values from -120 to 120
- index_query: bfloat16 [256, 8192], P('ctx', 'hg'), may hold values from -8 to 8
- index_weight: bfloat16 [256, 64], P('ctx', 'hg'), may hold values from 0.099609375 to 1
- main_nope: bfloat16 [65536, 16384], P('ctx', 'hg'), may hold values from -6 to 6
- main_rope: bfloat16 [65536, 64], P('ctx'), may hold values from -6 to 6
- index_keys: bfloat16 [65536, 128], P('ctx'), may hold values from -6 to 6
- query_pos: int32 [256], replicated, may hold values from 0 to 65535, as said below
- query_seg: int32 [256], replicated, may hold values from 0 to 7, as said below
- key_pos: int32 [65536], P('ctx'), may hold values from 0 to 65535, as said below
- key_seg: int32 [65536], P('ctx'), may hold values from 0 to 7, as said below
- loss_weight: float32 [256], replicated, may hold values from 4 to 40
Outputs:
- index_query_grad: float32 [256, 8192], P('ctx', 'hg')
- index_key_grad: float32 [65536, 128], P('ctx')
- query_loss: float32 [256], P('hg')
The draws below stay inside these ranges and needn't reach their ends.
Inputs may be any that keep to these rules, and one draw needn't show every extreme that they name: `key_pos`: a permutation of the positions 0 to 65535. `query_pos`: 256 distinct positions below 65536, among them 0 and 65535. `key_seg`: documents are runs of consecutive positions numbered from 0 upward, max(8, 2) of them; the document of the key at that position. `query_seg`: the document of the query's position, numbered as for key_seg.
All inputs are finite; a program needn't handle non-finite values.
Results may differ from the reference program's by a relative error of at most 0.007.
Values may be sent and summed in bfloat16 or wider, within the bound.
A program may use at most 192 MiB of HBM per device.

```python
import math
import jax
import jax.numpy as jnp
from jax import lax

H = 128
DN = 128
DR = 64
HI = 64
DI = 128
QK = 192
QN = 256
KEY_DEV = 1024
CTX = 65536


def layout(key):
    key_order = jax.random.permutation(jax.random.fold_in(key, 101), CTX).astype(jnp.int32)
    doc_count = max(CTX // (8 * KEY_DEV), 2)
    cuts = (jax.random.permutation(jax.random.fold_in(key, 102), CTX - 1)[:doc_count - 1] + 1).astype(jnp.int32)
    starts = jnp.zeros((CTX,), jnp.int32).at[cuts].set(1)
    starts = starts.at[0].set(1)
    documents = (jnp.cumsum(starts) - 1).astype(jnp.int32)
    inner = (jax.random.permutation(jax.random.fold_in(key, 103), CTX - 2)[:QN - 2] + 1).astype(jnp.int32)
    listed = jnp.concatenate([jnp.array([0, CTX - 1], jnp.int32), inner])
    shuffle = jax.random.permutation(jax.random.fold_in(key, 106), QN)
    query_order = listed[shuffle].astype(jnp.int32)
    picked = jax.random.randint(jax.random.fold_in(key, 104), (QN,), 0, 16) == 0
    row_of = jnp.zeros((CTX,), jnp.int32).at[key_order].set(jnp.arange(CTX, dtype=jnp.int32))
    return (key_order, documents[key_order], query_order, documents[query_order], picked, row_of)


def value_block(key, salt, count, width):
    normal_part = jnp.clip(jax.random.normal(jax.random.fold_in(key, salt), (count, width), jnp.float32), -4.0, 4.0)
    return normal_part


def add_twins(values, key):
    key_order, key_docs, query_order, query_docs, picked, row_of = layout(key)
    prev_rows = row_of[jnp.maximum(query_order - 1, 0)]
    use = picked & (query_order > 0)
    target_rows = jnp.where(use, prev_rows, CTX)
    fresh = values[prev_rows]
    return values.at[target_rows].set(fresh, mode='drop')


def main_table(key):
    drawn = value_block(key, 120, CTX, H * DN)
    rotary = value_block(key, 130, CTX, DR)
    full = jnp.concatenate([drawn, rotary], axis=1)
    return add_twins(full, key)


def index_table(key):
    values = value_block(key, 140, CTX, DI)
    return add_twins(values, key)


def draw_main_nope(key, part):
    table = main_table(key)
    return table[:, :H * DN].astype(jnp.bfloat16)


def draw_main_rope(key, part):
    table = main_table(key)
    return table[:, H * DN:].astype(jnp.bfloat16)


def draw_index_keys(key, part):
    table = index_table(key)
    return table.astype(jnp.bfloat16)


def draw_main_query(key, part):
    own = jax.random.fold_in(key, 11)
    base = 2.0 * value_block(own, 150, QN, H * QK)
    return base.astype(jnp.bfloat16)


def draw_index_query(key, part):
    own = jax.random.fold_in(key, 12)
    base = value_block(own, 160, QN, HI * DI)
    return base.astype(jnp.bfloat16)


def draw_key_pos(key, part):
    return layout(key)[0]


def draw_key_seg(key, part):
    return layout(key)[1]


def draw_query_pos(key, part):
    return layout(key)[2]


def draw_query_seg(key, part):
    return layout(key)[3]


def levels(rng, shape, split, smallest, high):
    def one(dim, parts):
        heights = jax.random.uniform(jax.random.fold_in(jax.random.fold_in(rng, 6), dim), (parts,), jnp.float32, smallest / len(split), high / len(split))
        return jnp.repeat(jnp.exp(heights), shape[dim] // parts).reshape((-1,) + (1,) * (len(shape) - dim - 1))

    gain = one(*split[0])
    for cut in split[1:]:
        gain = gain * one(*cut)
    return gain


def setup_inputs(seed: int = 0) -> dict:
    splits = jax.random.split(jax.random.key(seed), 12)
    main_query = draw_main_query(jax.random.fold_in(splits[11], 71), 0)
    index_query = draw_index_query(jax.random.fold_in(splits[11], 71), 0)
    index_weight = jnp.clip(jnp.exp(math.log(1.0) - 2.306499 * jax.random.uniform(splits[2], (QN, HI), jnp.float32) ** levels(splits[2], (QN, HI), ((0, 64), (1, 4)), -0.2, 0.2)), 0.099609375, 1.0).astype(jnp.bfloat16)
    main_nope = draw_main_nope(jax.random.fold_in(splits[11], 71), 0)
    main_rope = draw_main_rope(jax.random.fold_in(splits[11], 71), 0)
    index_keys = draw_index_keys(jax.random.fold_in(splits[11], 71), 0)
    query_pos = draw_query_pos(jax.random.fold_in(splits[11], 71), 0)
    query_seg = draw_query_seg(jax.random.fold_in(splits[11], 71), 0)
    key_pos = draw_key_pos(jax.random.fold_in(splits[11], 71), 0)
    key_seg = draw_key_seg(jax.random.fold_in(splits[11], 71), 0)
    loss_weight = jnp.clip(jnp.exp(jax.random.uniform(splits[10], (QN,), jnp.float32, math.log(4.0), math.log(40.0))), 4.0, 40.0)
    return {"main_query": main_query, "index_query": index_query, "index_weight": index_weight, "main_nope": main_nope, "main_rope": main_rope, "index_keys": index_keys, "query_pos": query_pos, "query_seg": query_seg, "key_pos": key_pos, "key_seg": key_seg, "loss_weight": loss_weight}


def reference(main_query, index_query, index_weight, main_nope, main_rope, index_keys, query_pos, query_seg, key_pos, key_seg, loss_weight):
    allowed = (key_pos[None, :] <= query_pos[:, None]) & (key_seg[None, :] == query_seg[:, None])
    floor_value = jnp.float32(-1e+30)

    def main_head(total, head):
        block = lax.dynamic_slice_in_dim(main_query, head * QK, QK, 1)
        plain = lax.dynamic_slice_in_dim(main_nope, head * DN, DN, 1)
        score = jnp.dot(block[:, :DN], plain.T, preferred_element_type=jnp.float32)
        score = score + jnp.dot(block[:, DN:], main_rope.T, preferred_element_type=jnp.float32)
        score = score / math.sqrt(QK)
        masked = jnp.where(allowed, score, floor_value)
        peak = lax.optimization_barrier(jnp.max(masked, axis=1, keepdims=True))
        expo = jnp.where(allowed, jnp.exp(masked - peak), jnp.float32(0.0))
        return (total + expo / lax.optimization_barrier(jnp.sum(expo, axis=1, keepdims=True)), None)
    start = jnp.zeros((QN, CTX), jnp.float32)
    total, unused = lax.scan(main_head, start, jnp.arange(H, dtype=jnp.int32))
    target = total / H
    weights = index_weight.astype(jnp.float32)

    def index_head(acc, head):
        block = lax.dynamic_slice_in_dim(index_query, head * DI, DI, 1)
        dots = jnp.dot(block, index_keys.T, preferred_element_type=jnp.float32)
        weight_col = lax.dynamic_slice_in_dim(weights, head, 1, 1)
        return (acc + weight_col * jnp.maximum(dots, 0.0), None)
    acc, unused = lax.scan(index_head, start, jnp.arange(HI, dtype=jnp.int32))
    logits = acc / math.sqrt(DI)
    masked = jnp.where(allowed, logits, floor_value)
    peak = lax.optimization_barrier(jnp.max(masked, axis=1))
    expo = jnp.where(allowed, jnp.exp(masked - peak[:, None]), jnp.float32(0.0))
    log_norm = peak + jnp.log(lax.optimization_barrier(jnp.sum(expo, axis=1)))
    cross = lax.optimization_barrier(jnp.sum(target * logits, axis=1))
    query_loss = loss_weight * (log_norm - cross)
    dlogit = loss_weight[:, None] * (jnp.where(allowed, jnp.exp(logits - log_norm[:, None]), jnp.float32(0.0)) - target)

    def back_head(key_acc, head):
        block = lax.dynamic_slice_in_dim(index_query, head * DI, DI, 1)
        dots = jnp.dot(block, index_keys.T, preferred_element_type=jnp.float32)
        weight_col = lax.dynamic_slice_in_dim(weights, head, 1, 1)
        dscore = (dlogit * weight_col * (dots > 0).astype(jnp.float32) / math.sqrt(DI)).astype(jnp.bfloat16)
        query_part = jnp.dot(dscore, index_keys, preferred_element_type=jnp.float32)
        key_acc = key_acc + jnp.dot(dscore.T, block, preferred_element_type=jnp.float32)
        return (key_acc, query_part)
    key_start = jnp.zeros((CTX, DI), jnp.float32)
    index_key_grad, query_parts = lax.scan(back_head, key_start, jnp.arange(HI, dtype=jnp.int32))
    index_query_grad = jnp.transpose(query_parts, (1, 0, 2)).reshape(QN, HI * DI)
    return (index_query_grad, index_key_grad, query_loss)
```

```python
import functools
import math

import jax
import jax.numpy as jnp
from jax import lax
from jax.experimental import pallas as pl
from jax.experimental.pallas import tpu as pltpu
from jax.sharding import PartitionSpec as P

MESH = pl.DeviceIdType.MESH
F32 = jnp.float32
BF16 = jnp.bfloat16
DN = 128
DR = 64
DI = 128
QK = 192
H = 128
QN = 256
KEYS = 1024
BLK = 256
IC = 512
MC = 1536
CW = IC + MC + 128
HEADS = 32
LOG2E = math.log2(math.e)
NEG = -1e30

S_GROUP, S_Z, S_R1, S_R2, S_SIB = 0, 3, 4, 8, 24
S_LOGIT, S_LN, S_LSE, S_PROB, S_DL, S_CROSS = 40, 43, 46, 54, 57, 60
S_KRS, S_KAG, S_GSIB, S_GREL, S_GR1, S_GR2, S_GZ, S_GGRP = 71, 74, 77, 79, 83, 91, 94, 95
N_SEM = 98


def dot_tt(a, b):
    return lax.dot_general(a, b, (((1,), (1,)), ((), ())), preferred_element_type=F32)


def dot_nn(a, b):
    return lax.dot_general(a, b, (((1,), (0,)), ((), ())), preferred_element_type=F32)


def kernel(
    pack_ref, ik_ref, rope_ref, kcode_ref, qv_ref, lw_ref, nope_hbm,
    oq_ref, ok_ref, oloss_ref,
    ssem, rsem, lsem,
    gbuf, gasm, G, KV, bias, W, KT, L, LB, LQ, LNS, LNB,
    E, M, SUM, XS, XSIB, XX, XY, XZ, PS, PB, TQ, DL, CS, CHG, CSIB, CX, CY, CZ,
    KA, KS, KB, KG, T, RB, U, RL, RR, V, VB, VZ, YB, OB,
):
    me = lax.axis_index("ctx")
    hg = lax.axis_index("hg")
    c = lax.rem(me, 2)
    x = lax.rem(me // 2, 4)
    z = lax.rem(me // 8, 2)
    y = me // 16
    xb, xp = lax.rem(x, 2), x // 2
    q = xb * 2 + c
    first = c == 0

    def cid(yy, zz, xx, cc):
        return ((yy * 2 + zz) * 4 + xx) * 2 + cc

    def mod4(v):
        return lax.rem(v + 4, 4)

    sib = (cid(y, z, x, 1 - c), hg)
    xo = x + 1 - 2 * xb
    group = [
        (xb * 2 + 1 - c, sib),
        ((1 - xb) * 2 + c, (cid(y, z, xo, c), hg)),
        ((1 - xb) * 2 + 1 - c, (cid(y, z, xo, 1 - c), hg)),
    ]
    zdev = (cid(y, 1 - z, x, c), hg)
    xdev = {s: (cid(y, z, mod4(x + s), c), hg) for s in (1, -1, 2)}
    ydev = {s: (cid(mod4(y + s), z, x, c), hg) for s in (1, -1, 2)}
    hdev = {s: (me, mod4(hg + s)) for s in (1, 2, 3)}
    r1 = {s: (jnp.where(first, xdev[s][0], ydev[s][0]), hg) for s in (1, -1, 2)}
    r2 = {s: (jnp.where(first, ydev[s][0], xdev[s][0]), hg) for s in (1, -1, 2)}

    started = []

    def send(src, dst, k, dev):
        cp = pltpu.make_async_remote_copy(
            src_ref=src, dst_ref=dst, send_sem=ssem.at[k], recv_sem=rsem.at[k],
            device_id=dev, device_id_type=MESH,
        )
        cp.start()
        started.append(cp)
        return cp

    loads = []
    for i in range(4):
        cols = pl.ds(i * 1024, 1024)
        cp = pltpu.make_async_copy(nope_hbm.at[:, cols], KV.at[:, cols], lsem.at[i])
        cp.start()
        loads.append(cp)

    barrier = pltpu.get_barrier_semaphore()
    partners = [sib, group[1][1], group[2][1], zdev, xdev[2], hdev[1], hdev[2], hdev[3]]
    partners += [ydev[s] for s in (1, -1, 2)]
    xn = (cid(y, z, mod4(x - 1 + 2 * xb), c), hg)
    partners.append(xn)
    for dev in partners:
        pl.semaphore_signal(barrier, inc=1, device_id=dev, device_id_type=MESH)
    pl.semaphore_wait(barrier, len(partners))

    cps = [
        send(pack_ref.at[g], gbuf.at[q], S_GROUP + i, dev) for i, (g, dev) in enumerate(group)
    ]
    gbuf[q] = pack_ref[q]

    kcode = kcode_ref[...]
    ok = (kcode >= qv_ref[0:1, :]) & (kcode <= qv_ref[1:2, :])
    bias[...] = jnp.where(ok, 0.0, NEG).astype(F32)
    KT[...] = jnp.transpose(ik_ref[...].astype(F32)).astype(BF16)

    for cp in cps:
        cp.wait_recv()
    for s in range(4):
        gasm[4 * s : 4 * s + 4, :] = gbuf[s]

    def unit(ch, yy, xx):
        return G.at[ch, pl.ds(pl.multiple_of((yy * 2 + xx) * 32, 32), 32), :]

    def half(ch, yy, xx, zz):
        return G.at[ch, pl.ds(pl.multiple_of(((yy * 2 + xx) * 2 + zz) * 16, 16), 16), :]

    own_rows = pl.multiple_of(((y * 2 + xp) * 2 + z) * 16, 16)
    G[q, pl.ds(own_rows, 16), :] = gasm[...].astype(BF16)
    own_half = half(q, y, xp, z)
    cpz = send(own_half, own_half, S_Z, zdev)

    def r1_coord(s):
        xx, yy = mod4(x + s), mod4(y + s)
        return (
            jnp.where(first, lax.rem(xx, 2) * 2 + c, q),
            jnp.where(first, y, yy),
            jnp.where(first, xx // 2, xp),
        )

    def r2_coord(s, k):
        xx = jnp.where(first, mod4(x + k), mod4(x + s))
        yy = jnp.where(first, mod4(y + s), mod4(y + k))
        return (lax.rem(xx, 2) * 2 + c, yy, xx // 2)

    sib_cps = []

    def to_sib(co):
        u = unit(*co)
        sib_cps.append(send(u, u, S_SIB + len(sib_cps), sib))

    offs = (0, -1, 1, 2)
    r2p, r2m = {}, {}

    def to_r2(k):
        u = unit(*r1_coord(offs[k]))
        r2p[k] = send(u, u, S_R2 + k, r2[1])
        r2m[k] = send(u, u, S_R2 + 4 + k, r2[-1])

    cpz.wait_recv()
    cpz.wait_send()
    u0 = unit(*r1_coord(0))
    cp_p = send(u0, u0, S_R1, r1[1])
    cp_m = send(u0, u0, S_R1 + 1, r1[-1])
    to_r2(0)
    to_sib(r1_coord(0))
    cp_p.wait_recv()
    h = half(*r1_coord(-1), 0)
    cp_fp = send(h, h, S_R1 + 2, r1[1])
    to_r2(1)
    cp_m.wait_recv()
    h = half(*r1_coord(1), 1)
    cp_fm = send(h, h, S_R1 + 3, r1[-1])
    to_r2(2)
    to_sib(r1_coord(-1))
    to_sib(r1_coord(1))
    cp_fp.wait_recv()
    cp_fm.wait_recv()
    to_r2(3)
    to_sib(r1_coord(2))
    fwd = []
    for k in range(4):
        r2p[k].wait_recv()
        co = r2_coord(-1, offs[k])
        if k < 2:
            fwd.append(send(unit(*co), unit(*co), S_R2 + 8 + k, r2[1]))
        to_sib(co)
        r2m[k].wait_recv()
        co = r2_coord(1, offs[k])
        if k >= 2:
            fwd.append(send(unit(*co), unit(*co), S_R2 + 8 + k, r2[-1]))
        to_sib(co)
    for k in range(4):
        fwd[k].wait_recv()
        to_sib(r2_coord(2, offs[k]))
    for cp in sib_cps:
        cp.wait_recv()

    def index_chunk(ch, carry):
        w = jnp.transpose(G[ch, :, IC + MC : CW].astype(F32))
        W[ch] = w[0:8, :] * (1.0 / math.sqrt(DI))
        for b in range(4):
            acc = jnp.zeros((BLK, QN), F32)
            for j in range(4):
                d = dot_tt(ik_ref[b * BLK : (b + 1) * BLK, :], G[ch, :, j * DI : (j + 1) * DI])
                acc = acc + jnp.maximum(d, 0.0) * W[ch, j : j + 1, :]
            L[b] = L[b] + acc
        return carry

    L[...] = jnp.zeros(L.shape, F32)
    lax.fori_loop(0, 4, index_chunk, 0)
    lcps = [send(L.at[mod4(hg + s)], LB.at[s - 1], S_LOGIT + s - 1, hdev[s]) for s in (1, 2, 3)]

    for cp in loads:
        cp.wait()

    scale = LOG2E / math.sqrt(QK)

    def main_pair(p, carry):
        ch = p // 4
        off = IC + lax.rem(p, 4) * 384
        qr = G[ch, :, pl.ds(pl.multiple_of(off + 256, 128), 128)]
        for i in range(2):
            hd = 2 * p + i
            qn = G[ch, :, pl.ds(pl.multiple_of(off + i * 128, 128), 128)]
            rhs = jnp.concatenate([qn, qr], axis=1)
            kcols = pl.ds(pl.multiple_of(hd * DN, 128), DN)
            for b in range(4):
                rows = slice(b * BLK, (b + 1) * BLK)
                lhs = jnp.concatenate(
                    [KV[rows, kcols], rope_ref[rows, i * 128 : (i + 1) * 128]], axis=1
                )
                s = dot_tt(lhs, rhs) * scale + bias[rows, :]
                m = jnp.max(s, axis=0, keepdims=True)
                e = jnp.exp2(s - m)
                M[b, pl.ds(hd, 1), :] = m
                SUM[b, pl.ds(hd, 1), :] = jnp.sum(e, axis=0, keepdims=True)
                E[hd, rows, :] = e.astype(BF16)
        return carry

    lax.fori_loop(0, 8, main_pair, 0)

    for cp in lcps:
        cp.wait_recv()
    lq = L[hg] + LB[0] + LB[1] + LB[2]
    LQ[...] = lq
    qrows = pl.ds(pl.multiple_of(hg * BLK, BLK), BLK)
    l2 = lq * LOG2E + bias[qrows, :]
    m = jnp.max(l2, axis=0, keepdims=True)
    part = m + jnp.log2(jnp.sum(jnp.exp2(l2 - m), axis=0, keepdims=True))
    LNS[...] = jnp.broadcast_to(part, (8, QN))
    ncps = [send(LNS, LNB.at[s - 1], S_LN + s - 1, hdev[s]) for s in (1, 2, 3)]

    lax.fori_loop(8, 16, main_pair, 0)

    def lse(parts):
        top = functools.reduce(jnp.maximum, parts)
        tot = functools.reduce(jnp.add, [jnp.exp2(v - top) for v in parts])
        return top + jnp.log2(tot)

    mm = jnp.maximum(jnp.maximum(M[0], M[1]), jnp.maximum(M[2], M[3]))
    ss = sum(SUM[b] * jnp.exp2(M[b] - mm) for b in range(4))
    XS[0, 0:HEADS, :] = mm + jnp.log2(ss)
    for cp in ncps:
        cp.wait_recv()
    XS[0, HEADS : HEADS + 8, :] = lse([LNS[...], LNB[0], LNB[1], LNB[2]])

    cp = send(XS.at[0], XSIB, S_LSE, sib)
    cp.wait_recv()
    XS[1] = lse([XS[0], XSIB[...]])
    cps = [send(XS.at[1], XX.at[i], S_LSE + 1 + i, xdev[s]) for i, s in enumerate((1, -1, 2))]
    for cp in cps:
        cp.wait_recv()
    XS[2] = lse([XS[1], XX[0], XX[1], XX[2]])
    cps = [send(XS.at[2], XY.at[i], S_LSE + 4 + i, ydev[s]) for i, s in enumerate((1, -1, 2))]
    for cp in cps:
        cp.wait_recv()
    XS[3] = lse([XS[2], XY[0], XY[1], XY[2]])
    cp = send(XS.at[3], XZ, S_LSE + 7, zdev)
    cp.wait_recv()
    XS[4] = lse([XS[3], XZ[...]])

    for b in range(4):
        M[b] = jnp.exp2(M[b] - XS[4, 0:HEADS, :])

    def head_sum(t, put):
        def sub(i, carry):
            rows = pl.ds(pl.multiple_of(t * BLK + i * 64, 64), 64)
            acc = jnp.zeros((64, QN), F32)
            for hd in range(HEADS):
                acc = acc + E[hd, rows, :].astype(F32) * M[t, hd : hd + 1, :]
            put(pl.ds(pl.multiple_of(i * 64, 64), 64), acc)
            return carry

        lax.fori_loop(0, 4, sub, 0)

    pcps = []
    for s in (1, 2, 3):
        t = mod4(hg + s)

        def put_out(rows, acc, t=t):
            PS[t, rows, :] = acc.astype(BF16)

        head_sum(t, put_out)
        pcps.append(send(PS.at[t], PB.at[s - 1], S_PROB + s - 1, hdev[s]))

    def put_own(rows, acc):
        TQ[rows, :] = acc

    head_sum(hg, put_own)
    for cp in pcps:
        cp.wait_recv()

    target = (
        TQ[...] + PB[0].astype(F32) + PB[1].astype(F32) + PB[2].astype(F32)
    ) * (1.0 / H)
    norm2 = XS[4, HEADS : HEADS + 1, :]
    lq = LQ[...]
    prob = jnp.exp2(lq * LOG2E + bias[qrows, :] - norm2)
    DL[hg] = (lw_ref[0:1, :] * (prob - target)).astype(BF16)
    dcps = [send(DL.at[hg], DL.at[hg], S_DL + s - 1, hdev[s]) for s in (1, 2, 3)]
    cross = jnp.sum(target * lq, axis=0, keepdims=True)
    CS[0] = jnp.broadcast_to(cross, (8, QN))
    ccps = [send(CS.at[0], CHG.at[s - 1], S_CROSS + s - 1, hdev[s]) for s in (1, 2, 3)]
    for cp in ccps + dcps:
        cp.wait_recv()
    CS[1] = CS[0] + CHG[0] + CHG[1] + CHG[2]
    cp_c = send(CS.at[1], CSIB, S_CROSS + 3, sib)

    KA[...] = jnp.zeros(KA.shape, F32)

    def grad_chunk(ch, carry):
        for j in range(4):
            qj = G[ch, :, j * DI : (j + 1) * DI]
            wj = W[ch, j : j + 1, :]
            tt = jnp.zeros((DI, QN), F32)
            for b in range(4):
                d = dot_tt(ik_ref[b * BLK : (b + 1) * BLK, :], qj)
                ds = jnp.where(d > 0, DL[b].astype(F32) * wj, 0.0).astype(BF16)
                KA[b] = KA[b] + dot_nn(ds, qj)
                tt = tt + dot_nn(KT[:, b * BLK : (b + 1) * BLK], ds)
            T[ch, :, j * DI : (j + 1) * DI] = jnp.transpose(tt)
        return carry

    lax.fori_loop(0, 4, grad_chunk, 0)

    KS[...] = KA[...].astype(BF16)
    kcps = [send(KS.at[mod4(hg + s)], KB.at[s - 1], S_KRS + s - 1, hdev[s]) for s in (1, 2, 3)]
    gcps = [send(T.at[2 * k + 1 - c], RB.at[k], S_GSIB + k, sib) for k in range(2)]

    cp_c.wait_recv()
    CS[2] = CS[1] + CSIB[...]
    ccps = [send(CS.at[2], CX.at[i], S_CROSS + 4 + i, xdev[s]) for i, s in enumerate((1, -1, 2))]

    for k in range(2):
        gcps[k].wait_recv()
        U[k] = T[2 * k + c] + RB[k]

    def uref(s, k):
        xx = jnp.where(first, k, mod4(x + s))
        yy = jnp.where(first, mod4(y + s), k)
        return U.at[
            lax.rem(xx, 2), pl.ds(pl.multiple_of((yy * 2 + xx // 2) * 32, 32), 32), :
        ]

    rel = [
        send(uref(2, k), RL.at[k], S_GREL + k, r2[1] if k < 2 else r2[-1]) for k in range(4)
    ]
    for cp in ccps:
        cp.wait_recv()
    CS[3] = CS[2] + CX[0] + CX[1] + CX[2]
    ccps = [send(CS.at[3], CY.at[i], S_CROSS + 7 + i, ydev[s]) for i, s in enumerate((1, -1, 2))]

    rp = [send(uref(1, k), RR.at[0, k], S_GR1 + k, r2[1]) for k in (2, 3)]
    rm = [send(uref(-1, k), RR.at[1, k], S_GR1 + 4 + k, r2[-1]) for k in (0, 1)]
    for k in range(4):
        rel[k].wait_recv()
        u = uref(1 if k < 2 else -1, k)
        u[...] = u[...] + RL[k]
        if k < 2:
            rp.append(send(u, RR.at[0, k], S_GR1 + k, r2[1]))
        else:
            rm.append(send(u, RR.at[1, k], S_GR1 + 4 + k, r2[-1]))

    for cp in kcps:
        cp.wait_recv()
    KG[hg] = KA[hg] + KB[0].astype(F32) + KB[1].astype(F32) + KB[2].astype(F32)
    kcps = [send(KG.at[hg], KG.at[hg], S_KAG + s - 1, hdev[s]) for s in (1, 2, 3)]

    for cp in ccps:
        cp.wait_recv()
    CS[4] = CS[3] + CY[0] + CY[1] + CY[2]
    cp_c = send(CS.at[4], CZ, S_CROSS + 10, zdev)

    for cp in rp + rm:
        cp.wait_recv()
    for k in range(4):
        V[k] = uref(0, k)[...] + RR[0, k] + RR[1, k]

    me1 = jnp.where(first, x, y)
    cps = [
        send(V.at[mod4(me1 + s)], VB.at[i], S_GR2 + i, r1[s]) for i, s in enumerate((1, -1, 2))
    ]
    for cp in cps:
        cp.wait_recv()
    VZ[0] = V[me1] + VB[0] + VB[1] + VB[2]
    cp = send(
        VZ.at[0, pl.ds(pl.multiple_of((1 - z) * 16, 16), 16), :], VZ.at[1, 0:16, :], S_GZ, zdev
    )
    cp_c.wait_recv()
    tot = CS[4] + CZ[...]
    oloss_ref[...] = lw_ref[...] * (
        XS[4, HEADS : HEADS + 8, :] * (1.0 / LOG2E) - tot
    )
    cp.wait_recv()
    own = VZ[0, pl.ds(pl.multiple_of(z * 16, 16), 16), :] + VZ[1, 0:16, :]
    for s in range(4):
        YB[s] = own[4 * s : 4 * s + 4, :]
    cps = [send(YB.at[g], OB.at[q], S_GGRP + i, dev) for i, (g, dev) in enumerate(group)]
    OB[q] = YB[q]
    for cp in cps:
        cp.wait_recv()
    for s in range(4):
        oq_ref[:, s * IC : (s + 1) * IC] = OB[s]

    for cp in kcps:
        cp.wait_recv()
    for t in range(4):
        ok_ref[t * BLK : (t + 1) * BLK, :] = KG[t]
    for cp in started:
        if cp is not cpz:
            cp.wait_send()


def rows_in(v):
    return v.reshape(4, 2, 2, 16).transpose(0, 2, 1, 3).reshape(QN)


def per_device(
    main_query, index_query, index_weight, main_nope, main_rope, index_keys,
    query_pos, query_seg, key_pos, key_seg, loss_weight,
):
    mq = main_query.reshape(4, 4, 4, 2, QK)
    nope = mq[..., :DN].reshape(4, 4, 4, 2 * DN)
    rope = mq[..., DN:].reshape(4, 4, 4, 2 * DR)
    main = jnp.concatenate([nope, rope], axis=-1).reshape(4, 4, MC)
    wts = jnp.pad(index_weight.reshape(4, 4, 4), ((0, 0), (0, 0), (0, 124)))
    pack = jnp.concatenate([index_query.reshape(4, 4, IC), main, wts], axis=-1)
    pack = pack.transpose(1, 0, 2).astype(F32)
    zero = jnp.zeros_like(main_rope)
    rope2 = jnp.concatenate([main_rope, zero, zero, main_rope], axis=1)
    kcode = (key_seg * 65536 + key_pos)[:, None]
    qlow = rows_in(query_seg * 65536)
    qhigh = rows_in(query_seg * 65536 + query_pos)
    qv = jnp.stack([qlow, qhigh] + [qlow] * 6)
    lw = jnp.broadcast_to(rows_in(loss_weight)[None], (8, QN))

    vm = pltpu.VMEM
    scratch = [
        pltpu.SemaphoreType.DMA((N_SEM,)),
        pltpu.SemaphoreType.DMA((N_SEM,)),
        pltpu.SemaphoreType.DMA((4,)),
        vm((4, 4, CW), F32),
        vm((16, CW), F32),
        vm((4, QN, CW), BF16),
        vm((KEYS, HEADS * DN), BF16),
        vm((KEYS, QN), F32),
        vm((4, 8, QN), F32),
        vm((DI, KEYS), BF16),
        vm((4, BLK, QN), F32),
        vm((3, BLK, QN), F32),
        vm((BLK, QN), F32),
        vm((8, QN), F32),
        vm((3, 8, QN), F32),
        vm((HEADS, KEYS, QN), BF16),
        vm((4, HEADS, QN), F32),
        vm((4, HEADS, QN), F32),
        vm((5, HEADS + 8, QN), F32),
        vm((HEADS + 8, QN), F32),
        vm((3, HEADS + 8, QN), F32),
        vm((3, HEADS + 8, QN), F32),
        vm((HEADS + 8, QN), F32),
        vm((4, BLK, QN), BF16),
        vm((3, BLK, QN), BF16),
        vm((BLK, QN), F32),
        vm((4, BLK, QN), BF16),
        vm((5, 8, QN), F32),
        vm((3, 8, QN), F32),
        vm((8, QN), F32),
        vm((3, 8, QN), F32),
        vm((3, 8, QN), F32),
        vm((8, QN), F32),
        vm((4, BLK, DI), F32),
        vm((4, BLK, DI), BF16),
        vm((3, BLK, DI), BF16),
        vm((4, BLK, DI), F32),
        vm((4, QN, IC), F32),
        vm((2, QN, IC), F32),
        vm((2, QN, IC), F32),
        vm((4, 32, IC), F32),
        vm((2, 4, 32, IC), F32),
        vm((4, 32, IC), F32),
        vm((3, 32, IC), F32),
        vm((2, 32, IC), F32),
        vm((4, 4, IC), F32),
        vm((4, 4, IC), F32),
    ]
    vspec = pl.BlockSpec(memory_space=pltpu.VMEM)
    index_query_grad, index_key_grad, loss = pl.pallas_call(
        kernel,
        out_shape=(
            jax.ShapeDtypeStruct((4, 4 * IC), F32),
            jax.ShapeDtypeStruct((KEYS, DI), F32),
            jax.ShapeDtypeStruct((8, QN), F32),
        ),
        in_specs=[vspec] * 6 + [pl.BlockSpec(memory_space=pl.ANY)],
        out_specs=(vspec, vspec, vspec),
        scratch_shapes=scratch,
        compiler_params=pltpu.CompilerParams(
            collective_id=0, has_side_effects=True, vmem_limit_bytes=58 * 1024 * 1024
        ),
    )(pack, index_keys, rope2, kcode, qv, lw, main_nope)
    full = loss[0].reshape(4, 2, 2, 16).transpose(0, 2, 1, 3).reshape(QN)
    share = QN // lax.axis_size("hg")
    query_loss = lax.dynamic_slice_in_dim(full, lax.axis_index("hg") * share, share, 0)
    return (index_query_grad, index_key_grad, query_loss)


def solution(mesh):
    return jax.shard_map(
        per_device,
        mesh=mesh,
        in_specs=(
            P("ctx", "hg"),
            P("ctx", "hg"),
            P("ctx", "hg"),
            P("ctx", "hg"),
            P("ctx", None),
            P("ctx", None),
            P(),
            P(),
            P("ctx"),
            P("ctx"),
            P(),
        ),
        out_specs=(P("ctx", "hg"), P("ctx", None), P("hg")),
        check_vma=False,
    )
```

```python
import functools
import math

import jax
import jax.numpy as jnp
from jax import lax
from jax.experimental import pallas as pl
from jax.experimental.pallas import tpu as pltpu
from jax.sharding import PartitionSpec as P

MESH = pl.DeviceIdType.MESH
F32 = jnp.float32
BF16 = jnp.bfloat16
DN = 128
DI = 128
QK = 192
PAIR = 2 * QK
H = 128
QN = 256
KEYS = 1024
BLK = 256
IC = 512
IW = IC + 128
MW = 2 * PAIR
HEADS = 32
HALF = HEADS // 2
G0 = HALF
LOG2E = math.log2(math.e)
NEG = -1e30
RING = (1, -1, 2)

S_AI, S_AM = 0, 7
S_WAVE = (14, 45, 76)
S_LOGIT, S_LNH, S_PROB, S_DL, S_CH = 107, 110, 113, 119, 125
S_LSE0, S_LSE1, S_LN, S_CR = 128, 136, 144, 161
S_KRS, S_KAG, S_GSIB, S_GPL, S_GFIN = 172, 178, 184, 186, 201
N_SEM = 208


def dot_tt(a, b):
    return lax.dot_general(a, b, (((1,), (1,)), ((), ())), preferred_element_type=F32)


def dot_nn(a, b):
    return lax.dot_general(a, b, (((1,), (0,)), ((), ())), preferred_element_type=F32)


def lse(parts):
    top = functools.reduce(jnp.maximum, parts)
    tot = functools.reduce(jnp.add, [jnp.exp2(v - top) for v in parts])
    return top + jnp.log2(tot)


def add(parts):
    return functools.reduce(jnp.add, parts)


def swap_rows(v):
    lane = lax.rem(lax.broadcasted_iota(jnp.int32, v.shape, 1), 64)
    up = pltpu.roll(v, QN - 16, 1)
    down = pltpu.roll(v, 16, 1)
    v = jnp.where((lane >= 16) & (lane < 32), up, v)
    return jnp.where((lane >= 32) & (lane < 48), down, v)


def kernel(
    mq_ref, iq_ref, iw_ref, rope_ref, ik_ref, kp_ref, ks_ref, qp_ref, qs_ref, lw_ref, nope_hbm,
    OB, KG, oloss_ref,
    ssem, rsem, lsem,
    FI, FM, SI, SM, RI, RM, XI, XM, AI, AM, GI, GM0, GM1, KV, ROPE, bias, W, LW, KT,
    L, LB, LNH, LNB,
    E, M, SUM, ES0, ES1, ESN, ESC, EB0, EB1, EBN, EBC, CH, CHB, PS, PB, PF, LQ, DL,
    KA, KS, KB, TT, T, RB, UB, VB, YB,
):
    me = lax.axis_index("ctx")
    hg = lax.axis_index("hg")
    c = lax.rem(me, 2)
    x = lax.rem(me // 2, 4)
    z = lax.rem(me // 8, 2)
    y = me // 16
    xb, xp = lax.rem(x, 2), x // 2
    q = xb * 2 + c
    slot = z * 4 + q
    first = c == 0

    def cid(yy, zz, xx, cc):
        return ((yy * 2 + zz) * 4 + xx) * 2 + cc

    def mod4(v):
        return lax.rem(v + 4, 4)

    octet = []
    for d in range(1, 8):
        cc = 1 - c if d % 2 else c
        bb = 1 - xb if d // 2 % 2 else xb
        zz = 1 - z if d // 4 else z
        octet.append((bb * 2 + cc, zz * 4 + bb * 2 + cc, (cid(y, zz, xp * 2 + bb, cc), hg)))
    sib = octet[0][2]
    zdev = octet[3][2]
    xdev = {s: (cid(y, z, mod4(x + s), c), hg) for s in RING}
    ydev = {s: (cid(mod4(y + s), z, x, c), hg) for s in RING}
    plane = {
        (dx, dy): (cid(mod4(y + dy), z, mod4(x + dx), c), hg)
        for dx in range(4) for dy in range(4) if (dx, dy) != (0, 0)
    }
    hdev = {s: (me, mod4(hg + s)) for s in (-3, -2, -1, 1, 2, 3)}
    r1 = {s: (jnp.where(first, xdev[s][0], ydev[s][0]), hg) for s in RING}
    r2 = {s: (jnp.where(first, ydev[s][0], xdev[s][0]), hg) for s in RING}

    started = []

    def send(src, dst, k, dev):
        cp = pltpu.make_async_remote_copy(
            src_ref=src, dst_ref=dst, send_sem=ssem.at[k], recv_sem=rsem.at[k],
            device_id=dev, device_id_type=MESH,
        )
        cp.start()
        started.append(cp)
        return cp

    loads = []
    for i in range(4):
        cols = pl.ds(i * 1024, 1024)
        cp = pltpu.make_async_copy(nope_hbm.at[:, cols], KV.at[:, cols], lsem.at[i])
        cp.start()
        loads.append(cp)

    barrier = pltpu.get_barrier_semaphore()
    partners = [dev for _, _, dev in octet if dev is not octet[1][2]]
    partners += list(plane.values()) + [hdev[s] for s in (1, 2, 3)]
    for dev in partners:
        pl.semaphore_signal(barrier, inc=1, device_id=dev, device_id_type=MESH)

    low = lax.broadcasted_iota(jnp.int32, (16, 128), 1) < 64
    FI[...] = jnp.zeros(FI.shape, F32)
    FI[16:20, 0:16] = iw_ref[...].astype(F32)
    for ch in range(4):
        for j in range(4):
            col = (ch * 4 + j) * DI
            FI[4 * j : 4 * j + 4, :] = iq_ref[:, col : col + DI].astype(F32)
        SI[ch] = FI[...].astype(BF16)
    pl.semaphore_wait(barrier, len(partners))

    a_i = [send(SI.at[g], RI.at[slot], S_AI + i, dev) for i, (g, _, dev) in enumerate(octet)]
    for ch in range(4):
        for p in range(4):
            col = (ch * 4 + p) * PAIR
            FM[4 * p : 4 * p + 4, :] = mq_ref[:, col : col + PAIR].astype(F32)
        t1, t2 = FM[:, 128:256], FM[:, 256:384]
        SM[ch, :, 0:128] = FM[:, 0:128].astype(BF16)
        SM[ch, :, 128:256] = jnp.where(
            low, pltpu.roll(t1, 64, 1), pltpu.roll(t2, 64, 1)
        ).astype(BF16)
        SM[ch, :, 256:384] = jnp.where(low, t1, t2).astype(BF16)
    a_m = [send(SM.at[g], RM.at[slot], S_AM + i, dev) for i, (g, _, dev) in enumerate(octet)]
    RI[slot] = SI[q]
    RM[slot] = SM[q]
    rows32 = pl.ds(pl.multiple_of((y * 2 + xp) * 32, 32), 32)
    for cp in a_i:
        cp.wait_recv()
    XI[...] = RI[...].astype(F32)
    for s in range(8):
        for j in range(5):
            AI[4 * s : 4 * s + 4, j * DI : (j + 1) * DI] = XI[s, 4 * j : 4 * j + 4, :]
    GI[q, rows32, :] = AI[...].astype(BF16)

    def r1_coord(s):
        xx, yy = mod4(x + s), mod4(y + s)
        return (
            jnp.where(first, lax.rem(xx, 2) * 2 + c, q),
            jnp.where(first, y, yy),
            jnp.where(first, xx // 2, xp),
        )

    def r2_coord(s, k):
        xx = jnp.where(first, mod4(x + k), mod4(x + s))
        yy = jnp.where(first, mod4(y + s), mod4(y + k))
        return (lax.rem(xx, 2) * 2 + c, yy, xx // 2)

    offs = (0, -1, 1, 2)

    def wave(G, base):
        s_r1, s_r2, s_sib = base, base + 3, base + 15
        sibs, one, two = [], {}, {}

        def unit(co):
            ch, yy, xx = co
            return G.at[ch, pl.ds(pl.multiple_of((yy * 2 + xx) * 32, 32), 32), :]

        def to_sib(co):
            u = unit(co)
            sibs.append(send(u, u, s_sib + len(sibs), sib))

        def to_two(k):
            u = unit(r1_coord(offs[k]))
            for i, s in enumerate(RING):
                two[s, k] = send(u, u, s_r2 + 3 * k + i, r2[s])

        u0 = unit(r1_coord(0))
        for i, s in enumerate(RING):
            one[s] = send(u0, u0, s_r1 + i, r1[s])
        to_sib(r1_coord(0))
        yield
        to_two(0)
        for k, s in ((1, 1), (2, -1), (3, 2)):
            one[s].wait_recv()
            to_two(k)
            to_sib(r1_coord(offs[k]))
        yield
        for s in RING:
            for k in range(4):
                two[s, k].wait_recv()
                to_sib(r2_coord(-s, offs[k]))
        yield
        for cp in sibs:
            cp.wait_recv()
        yield

    w_i = wave(GI, S_WAVE[0])
    next(w_i)
    for cp in a_m:
        cp.wait_recv()
    XM[...] = RM[...].astype(F32)
    for s in range(8):
        for p in range(4):
            AM[4 * s : 4 * s + 4, p * PAIR : (p + 1) * PAIR] = XM[s, 4 * p : 4 * p + 4, :]
    GM0[q, rows32, :] = AM[:, 0:MW].astype(BF16)
    GM1[q, rows32, :] = AM[:, MW : 2 * MW].astype(BF16)
    w_0 = wave(GM0, S_WAVE[1])
    w_1 = wave(GM1, S_WAVE[2])
    next(w_0)
    next(w_1)

    kcode = (ks_ref[...] * 65536 + kp_ref[...]).astype(F32)
    qcode = jnp.broadcast_to(qs_ref[...] * 65536, (8, QN)).astype(F32)
    qlow = swap_rows(qcode)[0:1, :]
    qhigh = swap_rows(qcode + jnp.broadcast_to(qp_ref[...], (8, QN)).astype(F32))[0:1, :]
    LW[...] = swap_rows(jnp.broadcast_to(lw_ref[...], (8, QN)))
    for r in range(8):
        col = jnp.transpose(jnp.broadcast_to(kcode[r : r + 1, :], (128, 128)))
        col = jnp.concatenate([col, col], axis=1)
        ok = (col >= qlow) & (col <= qhigh)
        bias[r * 128 : (r + 1) * 128, :] = jnp.where(ok, 0.0, NEG).astype(F32)
    next(w_i)
    next(w_0)
    next(w_1)
    for b in range(4):
        KT[b] = jnp.transpose(ik_ref[b * BLK : (b + 1) * BLK, :].astype(F32)).astype(BF16)
    rope = rope_ref[...].astype(F32)
    zero = jnp.zeros_like(rope)
    ROPE[:, 0:128] = jnp.transpose(jnp.concatenate([rope, zero], axis=0)).astype(BF16)
    ROPE[:, 128:256] = jnp.transpose(jnp.concatenate([zero, rope], axis=0)).astype(BF16)
    next(w_i)
    next(w_i)

    W[...] = jnp.transpose(GI[0, :, IC:IW].astype(F32))[0:16, :] * (1.0 / math.sqrt(DI))

    def index_part(t):
        trows = pl.ds(pl.multiple_of(t * BLK, BLK), BLK)
        L[t] = jnp.zeros((BLK, QN), F32)

        def chunk(ch, carry):
            acc = L[t]
            for j in range(4):
                d = dot_tt(ik_ref[trows, :], GI[ch, :, j * DI : (j + 1) * DI])
                acc = acc + jnp.maximum(d, 0.0) * W[pl.ds(4 * ch + j, 1), :]
            L[t] = acc
            return carry

        lax.fori_loop(0, 4, chunk, 0)

    lcps = []
    for s in (2, 1, 3):
        t = mod4(hg + s)
        index_part(t)
        lcps.append(send(L.at[t], LB.at[s - 1], S_LOGIT + s - 1, hdev[s]))
    index_part(hg)
    next(w_0)
    for cp in loads:
        cp.wait()
    next(w_0)

    scale = LOG2E / math.sqrt(QK)

    def main_pair(G, w, p, carry):
        ch = p // 2
        off = lax.rem(p, 2) * PAIR
        qr = G[ch, :, pl.ds(pl.multiple_of(off + 256, 128), 128)]
        for i in range(2):
            hd = w * HALF + 2 * p + i
            qn = G[ch, :, pl.ds(pl.multiple_of(off + i * 128, 128), 128)]
            rhs = jnp.concatenate([qn, qr], axis=1)
            kcols = pl.ds(pl.multiple_of((ch * 8 + w * 4 + lax.rem(p, 2) * 2 + i) * DN, 128), DN)
            for b in range(4):
                rows = slice(b * BLK, (b + 1) * BLK)
                lhs = jnp.concatenate(
                    [KV[rows, kcols], ROPE[rows, i * 128 : (i + 1) * 128]], axis=1
                )
                s = dot_tt(lhs, rhs) * scale + bias[rows, :]
                m = jnp.max(s, axis=0, keepdims=True)
                e = jnp.exp2(s - m)
                M[b, pl.ds(hd, 1), :] = m
                SUM[b, pl.ds(hd, 1), :] = jnp.sum(e, axis=0, keepdims=True)
                E[hd, rows, :] = e.astype(BF16)
        return carry

    pair0 = functools.partial(main_pair, GM0, 0)
    pair1 = functools.partial(main_pair, GM1, 1)

    def local_lse(a, b):
        r = slice(a, b)
        mm = functools.reduce(jnp.maximum, [M[i, r, :] for i in range(4)])
        ss = add([SUM[i, r, :] * jnp.exp2(M[i, r, :] - mm) for i in range(4)])
        return mm + jnp.log2(ss)

    def reduce_plane(S, B, base, combine):
        cp = send(S.at[0], B.at[0], base, sib)
        yield
        cp.wait_recv()
        S[1] = combine([S[0], B[0]])
        cps = [send(S.at[1], B.at[1 + i], base + 1 + i, dev) for i, dev in enumerate(plane.values())]
        yield
        for cp in cps:
            cp.wait_recv()
        S[3] = combine([S[1]] + [B[1 + i] for i in range(15)])
        cp = send(S.at[3], B.at[16], base + 16, zdev)
        yield
        cp.wait_recv()
        S[4] = combine([S[3], B[16]])
        yield

    def reduce_ctx(S, B, base, combine):
        cp = send(S.at[0], B.at[0], base, sib)
        yield
        cp.wait_recv()
        S[1] = combine([S[0], B[0]])
        cps = [send(S.at[1], B.at[1 + i], base + 1 + i, xdev[s]) for i, s in enumerate(RING)]
        yield
        for cp in cps:
            cp.wait_recv()
        S[2] = combine([S[1], B[1], B[2], B[3]])
        cps = [send(S.at[2], B.at[4 + i], base + 4 + i, ydev[s]) for i, s in enumerate(RING)]
        yield
        for cp in cps:
            cp.wait_recv()
        S[3] = combine([S[2], B[4], B[5], B[6]])
        cp = send(S.at[3], B.at[7], base + 7, zdev)
        yield
        cp.wait_recv()
        S[4] = combine([S[3], B[7]])
        yield

    lax.fori_loop(0, 6, pair0, 0)
    next(w_1)
    lax.fori_loop(6, 8, pair0, 0)
    ES0[0] = local_lse(0, G0)
    e_0 = reduce_ctx(ES0, EB0, S_LSE0, lse)
    next(e_0)
    next(w_1)
    lax.fori_loop(0, 6, pair1, 0)
    next(e_0)
    lax.fori_loop(6, 8, pair1, 0)
    ES1[0] = local_lse(G0, HEADS)
    e_1 = reduce_ctx(ES1, EB1, S_LSE1, lse)
    next(e_1)
    next(e_1)
    next(e_0)
    next(e_1)
    next(e_0)
    next(e_1)

    for cp in lcps:
        cp.wait_recv()
    lq = L[hg] + LB[0] + LB[1] + LB[2]
    LQ[...] = lq
    qrows = pl.ds(pl.multiple_of(hg * BLK, BLK), BLK)
    l2 = lq * LOG2E + bias[qrows, :]
    m = jnp.max(l2, axis=0, keepdims=True)
    part = m + jnp.log2(jnp.sum(jnp.exp2(l2 - m), axis=0, keepdims=True))
    LNH[...] = jnp.broadcast_to(part, (8, QN))
    ncps = [send(LNH, LNB.at[s - 1], S_LNH + s - 1, hdev[s]) for s in (1, 2, 3)]
    next(e_0)

    def head_sum(t, rows, n, acc, h0, h1):
        krows = pl.ds(pl.multiple_of(t * BLK + rows, 64), n)
        for hd in range(h0, h1):
            acc = acc + E[hd, krows, :].astype(F32) * M[t, hd : hd + 1, :]
        return acc

    for b in range(4):
        M[b, 0:G0, :] = jnp.exp2(M[b, 0:G0, :] - ES0[4])

    def sum_0(i, carry):
        t, rows = i // 4, lax.rem(i, 4) * 64
        PF[t, pl.ds(pl.multiple_of(rows, 64), 64), :] = head_sum(
            t, rows, 64, jnp.zeros((64, QN), F32), 0, G0
        )
        return carry

    lax.fori_loop(0, 16, sum_0, 0)
    for cp in ncps:
        cp.wait_recv()
    ESN[0] = lse([LNH[...], LNB[0], LNB[1], LNB[2]])
    e_n = reduce_plane(ESN, EBN, S_LN, lse)
    next(e_n)
    next(e_1)
    for b in range(4):
        M[b, G0:HEADS, :] = jnp.exp2(M[b, G0:HEADS, :] - ES1[4])

    def sum_1(t, u, own):
        def sub(i, carry):
            rows = u * 128 + i * 64
            here = pl.ds(pl.multiple_of(rows, 64), 64)
            acc = head_sum(t, rows, 64, PF[t, here, :], G0, HEADS)
            if own:
                PF[t, here, :] = acc
            else:
                PS[t, here, :] = acc.astype(BF16)
            return carry

        lax.fori_loop(0, 2, sub, 0)

    pcps = {}
    for u in range(2):
        part = slice(u * 128, (u + 1) * 128)
        for s in (2, 1, 3):
            t = mod4(hg + s)
            sum_1(t, u, False)
            pcps[u, s] = send(
                PS.at[t, part], PB.at[s - 1, part], S_PROB + 3 * u + s - 1, hdev[s]
            )
        if u == 0:
            next(e_n)
    for u in range(2):
        sum_1(hg, u, True)
    next(e_n)
    next(e_n)

    half = [slice(0, 128), slice(128, 256)]

    def grad_part(n, t, u, chunks):
        trows = pl.ds(pl.multiple_of(t * BLK + u * 128, 128), 128)

        def chunk(ch):
            qs = jnp.concatenate([GI[ch, :, j * DI : (j + 1) * DI] for j in range(4)], axis=0)
            d = dot_tt(ik_ref[trows, :], qs)
            dl = DL[t, half[u], :].astype(F32)
            ds = jnp.concatenate([
                jnp.where(
                    d[:, j * QN : (j + 1) * QN] > 0, dl * W[pl.ds(ch * 4 + j, 1), :], 0.0
                ).astype(BF16)
                for j in range(4)
            ], axis=1)
            KA[n, half[u], :] = KA[n, half[u], :] + dot_nn(ds, qs)
            tt = dot_nn(KT[t, :, half[u]], ds)
            if (n, u) == (0, 0):
                TT[ch] = tt
            elif (n, u) != (3, 1):
                TT[ch] = TT[ch] + tt
            else:
                tt = TT[ch] + tt
                for j in range(4):
                    T[ch, :, j * DI : (j + 1) * DI] = jnp.transpose(tt[:, j * QN : (j + 1) * QN])

        for ch in chunks:
            chunk(ch)

    KA[...] = jnp.zeros(KA.shape, F32)
    dcps = {}
    cross = jnp.zeros((1, QN), F32)
    for u in range(2):
        for s in (2, 1, 3):
            pcps[u, s].wait_recv()
        target = add([PF[hg, half[u], :]] + [PB[i, half[u], :].astype(F32) for i in range(3)])
        target = target * (1.0 / H)
        lq = LQ[half[u], :]
        brows = pl.ds(pl.multiple_of(hg * BLK + u * 128, 128), 128)
        prob = jnp.exp2(lq * LOG2E + bias[brows, :] - ESN[4, 0:1, :])
        DL[hg, half[u], :] = (LW[0:1, :] * (prob - target)).astype(BF16)
        for s in (2, 1, 3):
            mine = DL.at[hg, half[u]]
            dcps[u, s] = send(mine, mine, S_DL + 3 * u + s - 1, hdev[s])
        cross = cross + jnp.sum(target * lq, axis=0, keepdims=True)
        if u == 1:
            CH[...] = jnp.broadcast_to(cross, (8, QN))
            ccps = [send(CH, CHB.at[s - 1], S_CH + s - 1, hdev[s]) for s in (1, 2, 3)]
        grad_part(0, hg, u, range(4))

    kcps = {}
    order = (2, 1, 3)

    def key_out(n, u):
        KS[n - 1, half[u], :] = KA[n, half[u], :].astype(BF16)
        kcps[n, u] = send(
            KS.at[n - 1, half[u]], KB.at[n - 1, half[u]], S_KRS + 3 * u + n - 1, hdev[-order[n - 1]]
        )

    def key_sum(u):
        for n in (1, 2, 3):
            kcps[n, u].wait_recv()
        tot = KA[0, half[u], :] + add([KB[i, half[u], :].astype(F32) for i in range(3)])
        KG[hg, half[u], :] = tot.astype(BF16)
        mine = KG.at[hg, half[u]]
        return [send(mine, mine, S_KAG + 3 * u + s - 1, hdev[s]) for s in (2, 1, 3)]

    for u in range(2):
        for n in (1, 2, 3):
            if (n, u) == (3, 1):
                continue
            dcps[u, order[n - 1]].wait_recv()
            grad_part(n, mod4(hg - order[n - 1]), u, range(4))
            key_out(n, u)
            if (n, u) == (1, 1):
                next(e_c)
        if u == 0:
            for cp in ccps:
                cp.wait_recv()
            ESC[0] = add([CH[...], CHB[0], CHB[1], CHB[2]])
            e_c = reduce_ctx(ESC, EBC, S_CR, add)
            next(e_c)
    next(e_c)
    dcps[1, order[2]].wait_recv()

    turns = (1 - xb, xb)
    gcps = []
    for i, k in enumerate(turns):
        grad_part(3, mod4(hg - order[2]), 1, (2 * k, 2 * k + 1))
        gcps.append(send(T.at[2 * k + 1 - c], RB.at[k], S_GSIB + i, sib))
    key_out(3, 1)
    vcps = []
    for i, k in enumerate(turns):
        gcps[i].wait_recv()
        UB[k] = (T[2 * k + c] + RB[k]).astype(BF16)
        for dx in ((1, 3), (0, 2))[i]:
            for dy in (0, 1, 3, 2):
                if (dx, dy) == (0, 0):
                    continue
                n = dx * 4 + dy - 1
                xx, yy = mod4(x + dx), mod4(y + dy)
                urows = pl.ds(pl.multiple_of((yy * 2 + xx // 2) * 32, 32), 32)
                vcps.append(send(UB.at[k, urows], VB.at[n], S_GPL + n, plane[dx, dy]))
    own = T[q, rows32, :] + RB[xb, rows32, :]
    gkcps = key_sum(0)
    next(e_c)
    gkcps += key_sum(1)

    for cp in vcps:
        cp.wait_recv()
    own = own + add([VB[i].astype(F32) for i in range(15)])
    for s in range(8):
        YB[s] = own[4 * s : 4 * s + 4, :]
    cps = [
        send(YB.at[g], OB.at[slot], S_GFIN + i, dev) for i, (_, g, dev) in enumerate(octet)
    ]
    OB[slot] = YB[slot]
    next(e_c)
    loss = LW[...] * (ESN[4] * (1.0 / LOG2E) - ESC[4])
    oloss_ref[...] = pltpu.roll(swap_rows(loss), lax.rem(QN - 64 * hg, QN), 1)
    for cp in cps + gkcps:
        cp.wait_recv()
    for cp in started:
        cp.wait_send()


def finish(ob_ref, kg_ref, loss_ref, oq_ref, ok_ref, oloss_ref):
    for s in range(4):
        oq_ref[:, s * IC : (s + 1) * IC] = ob_ref[s] + ob_ref[4 + s]
    for t in range(4):
        ok_ref[t * BLK : (t + 1) * BLK, :] = kg_ref[t].astype(F32)
    oloss_ref[...] = loss_ref[0:1, 0:64]


def per_device(
    main_query, index_query, index_weight, main_nope, main_rope, index_keys,
    query_pos, query_seg, key_pos, key_seg, loss_weight,
):
    vm = pltpu.VMEM
    scratch = [
        pltpu.SemaphoreType.DMA((N_SEM,)),
        pltpu.SemaphoreType.DMA((N_SEM,)),
        pltpu.SemaphoreType.DMA((4,)),
        vm((32, DI), F32),
        vm((16, PAIR), F32),
        vm((4, 32, DI), BF16),
        vm((4, 16, PAIR), BF16),
        vm((8, 32, DI), BF16),
        vm((8, 16, PAIR), BF16),
        vm((8, 32, DI), F32),
        vm((8, 16, PAIR), F32),
        vm((32, IW), F32),
        vm((32, 2 * MW), F32),
        vm((4, QN, IW), BF16),
        vm((4, QN, MW), BF16),
        vm((4, QN, MW), BF16),
        vm((KEYS, HEADS * DN), BF16),
        vm((KEYS, 256), BF16),
        vm((KEYS, QN), F32),
        vm((16, QN), F32),
        vm((8, QN), F32),
        vm((4, DI, BLK), BF16),
        vm((4, BLK, QN), F32),
        vm((3, BLK, QN), F32),
        vm((8, QN), F32),
        vm((3, 8, QN), F32),
        vm((HEADS, KEYS, QN), BF16),
        vm((4, HEADS, QN), F32),
        vm((4, HEADS, QN), F32),
        vm((5, G0, QN), F32),
        vm((5, HEADS - G0, QN), F32),
        vm((5, 8, QN), F32),
        vm((5, 8, QN), F32),
        vm((8, G0, QN), F32),
        vm((8, HEADS - G0, QN), F32),
        vm((17, 8, QN), F32),
        vm((8, 8, QN), F32),
        vm((8, QN), F32),
        vm((3, 8, QN), F32),
        vm((4, BLK, QN), BF16),
        vm((3, BLK, QN), BF16),
        vm((4, BLK, QN), F32),
        vm((BLK, QN), F32),
        vm((4, BLK, QN), BF16),
        vm((4, BLK, DI), F32),
        vm((3, BLK, DI), BF16),
        vm((3, BLK, DI), BF16),
        vm((4, DI, 4 * QN), F32),
        vm((4, QN, IC), F32),
        vm((2, QN, IC), F32),
        vm((2, QN, IC), BF16),
        vm((15, 32, IC), BF16),
        vm((8, 4, IC), F32),
    ]
    vspec = pl.BlockSpec(memory_space=pltpu.VMEM)
    ob, kg, loss = pl.pallas_call(
        kernel,
        out_shape=(
            jax.ShapeDtypeStruct((8, 4, IC), F32),
            jax.ShapeDtypeStruct((4, BLK, DI), BF16),
            jax.ShapeDtypeStruct((8, QN), F32),
        ),
        in_specs=[vspec] * 10 + [pl.BlockSpec(memory_space=pl.ANY)],
        out_specs=(vspec, vspec, vspec),
        scratch_shapes=scratch,
        compiler_params=pltpu.CompilerParams(
            collective_id=0, has_side_effects=True, vmem_limit_bytes=58 * 1024 * 1024
        ),
    )(
        main_query, index_query, index_weight, main_rope.T, index_keys,
        key_pos.reshape(8, 128), key_seg.reshape(8, 128),
        query_pos.reshape(1, QN), query_seg.reshape(1, QN), loss_weight.reshape(1, QN),
        main_nope,
    )
    index_query_grad, index_key_grad, loss = pl.pallas_call(
        finish,
        out_shape=(
            jax.ShapeDtypeStruct((4, 4 * IC), F32),
            jax.ShapeDtypeStruct((KEYS, DI), F32),
            jax.ShapeDtypeStruct((1, 64), F32),
        ),
        in_specs=[vspec] * 3,
        out_specs=(vspec, vspec, vspec),
    )(ob, kg, loss)
    return (index_query_grad, index_key_grad, loss.reshape(64))


def solution(mesh):
    return jax.shard_map(
        per_device,
        mesh=mesh,
        in_specs=(
            P("ctx", "hg"),
            P("ctx", "hg"),
            P("ctx", "hg"),
            P("ctx", "hg"),
            P("ctx", None),
            P("ctx", None),
            P(),
            P(),
            P("ctx"),
            P("ctx"),
            P(),
        ),
        out_specs=(P("ctx", "hg"), P("ctx", None), P("hg")),
        check_vma=False,
    )
```
